32 devices in a mesh: member: 8 (over y, x, core), space: 4 (over z).
Axes of the slice: x: 2, y: 2, z: 4, core: 2. Of those that a mesh axis runs over, the one named last changes fastest.
Arguments:
- layer_input: bfloat16 [32, 1024, 256], P('member', 'space'), may hold values from -6 to 6
- out_grad: bfloat16 [32, 1024, 256], P('member', 'space'), may hold values from -6 to 6
- norm1_gain: float32 [256], replicated, as said below
- w_query: bfloat16 [256, 256], replicated, as said below
- w_key: bfloat16 [256, 256], replicated, as said below
- w_value: bfloat16 [256, 256], replicated, may hold values from -0.375 to 0.375
- w_out: bfloat16 [256, 256], replicated, may hold values from -0.375 to 0.375
- norm2_gain: float32 [256], replicated, may hold values from 0.5 to 1.5
- w_up: bfloat16 [256, 1024], replicated, may hold values from -0.375 to 0.375
- w_down: bfloat16 [1024, 256], replicated, may hold values from -0.1875 to 0.1875
Outputs:
- input_grad: float32 [32, 1024, 256], P('member', 'space')
- grad_query: float32 [256, 256], replicated
- grad_key: float32 [256, 256], replicated
- grad_value: float32 [256, 256], replicated
- grad_wout: float32 [256, 256], replicated
- grad_up: float32 [256, 1024], replicated
- grad_down: float32 [1024, 256], replicated
- grad_gain1: float32 [256], replicated
- grad_gain2: float32 [256], replicated
The draws below stay inside these ranges and needn't reach their ends.
Inputs may be any that keep to these rules, and one draw needn't show every extreme that they name: `norm1_gain`: positive gains, between 0.5 and 3. `w_query`: entries of a query projection. `w_key`: entries of a key projection.
All inputs are finite; a program needn't handle non-finite values.
Results may differ from the reference program's by a relative error of at most 0.008.
The reference program's roundings to bfloat16 on the way count: a program that leaves them out, or rounds other values in their place, can miss the bound.
Values may be sent and summed in bfloat16 or wider, within the bound.
A program may use at most 128 MiB of HBM per device.

```python
import math
import jax
import jax.numpy as jnp
from jax import lax

D = 256
HEAD_DIM = 32
FF = 1024
MEMBERS = 32
PATCHES = 1024


def shared_rows(key):
    base = jax.random.truncated_normal(jax.random.fold_in(key, 101), -3.0, 3.0, (D, D), jnp.float32) * D ** (-0.5)
    return base


def draw_w_query(key, part):
    base = shared_rows(key)
    return base.astype(jnp.bfloat16)


def draw_w_key(key, part):
    key = jax.random.fold_in(key, 7)
    own = jax.random.truncated_normal(key, -3.0, 3.0, (D, D), jnp.float32) * D ** (-0.5)
    return own.astype(jnp.bfloat16)


def draw_norm1_gain(key, part):
    key = jax.random.fold_in(key, 3)
    return jax.random.uniform(key, (D,), jnp.float32, 0.5, 1.5)


def block_levels(stream_key, shape, cuts, least, largest):
    def one(axis_at, blocks):
        heights = jax.random.uniform(jax.random.fold_in(jax.random.fold_in(stream_key, 6), axis_at), (blocks,), jnp.float32, least / len(cuts), largest / len(cuts))
        return jnp.repeat(jnp.exp(heights), shape[axis_at] // blocks).reshape((-1,) + (1,) * (len(shape) - axis_at - 1))

    level = one(*cuts[0])
    for cut in cuts[1:]:
        level = level * one(*cut)
    return level


def centred(rng, extent, spread, limit, cuts=(), held_as=jnp.bfloat16):
    gain = block_levels(rng, extent, cuts, -0.22, 0.18) if cuts else 1.0
    values = jax.random.normal(rng, extent, jnp.float32) * spread * gain
    return jnp.minimum(jnp.maximum(values, -limit), limit).astype(held_as)


def setup_inputs(seed: int = 0) -> dict:
    key_of = jax.random.split(jax.random.key(seed), 11)
    layer_input = centred(key_of[0], (MEMBERS, PATCHES, D), 1.0, 6.0, ((0, 8), (1, 4)))
    out_grad = centred(key_of[1], (MEMBERS, PATCHES, D), 1.0, 6.0, ((0, 8), (1, 4)))
    norm1_gain = draw_norm1_gain(jax.random.fold_in(key_of[10], 71), 0)
    w_query = draw_w_query(jax.random.fold_in(key_of[10], 71), 0)
    w_key = draw_w_key(jax.random.fold_in(key_of[10], 71), 0)
    w_value = centred(key_of[5], (D, D), D ** -0.5, 0.375)
    w_out = centred(key_of[6], (D, D), D ** -0.5, 0.375)
    norm2_gain = jnp.clip(1.0 + 0.1 * jax.random.normal(key_of[7], (D,), jnp.float32), 0.5, 1.5)
    w_up = centred(key_of[8], (D, FF), D ** -0.5, 0.375)
    w_down = centred(key_of[9], (FF, D), FF ** -0.5, 0.1875)
    return {"layer_input": layer_input, "out_grad": out_grad, "norm1_gain": norm1_gain, "w_query": w_query, "w_key": w_key, "w_value": w_value, "w_out": w_out, "norm2_gain": norm2_gain, "w_up": w_up, "w_down": w_down}


EPS = 1e-06
GELU_C = 0.7978845608028654
GELU_A = 0.044715

def multiply(form, left, right):
    return jnp.einsum(form, left.astype(jnp.float32), right.astype(jnp.float32))

def norm_rows(values):
    inverse = lax.rsqrt(lax.optimization_barrier(jnp.mean(values * values, axis=-1, keepdims=True)) + EPS)
    return (values * inverse, inverse)

def norm_back(unit_rows, inverse, gains, upstream):
    scaled = upstream * gains
    into = inverse * (scaled - unit_rows * lax.optimization_barrier(jnp.mean(scaled * unit_rows, axis=-1, keepdims=True)))
    return (into, lax.optimization_barrier(jnp.sum(upstream * unit_rows, axis=(0, 1))))

def gelu_pair(preact):
    tangent = jnp.tanh(GELU_C * (preact + GELU_A * preact * preact * preact))
    result = 0.5 * preact * (1.0 + tangent)
    slopes = 0.5 * (1.0 + tangent) + 0.5 * preact * (1.0 - tangent * tangent) * GELU_C * (1.0 + 3.0 * GELU_A * preact * preact)
    return (result, slopes)

def attend(query, keys, values, heads):
    members, count, width = query.shape
    shape_four = (members, count, heads, width // heads)
    scale = 1.0 / math.sqrt(width // heads)
    scores = multiply('mphe,nphe->phmn', query.reshape(shape_four), keys.reshape(shape_four)) * scale
    scores = scores - lax.optimization_barrier(jnp.max(scores, axis=-1, keepdims=True))
    weights = jnp.exp(scores)
    weights = weights / lax.optimization_barrier(jnp.sum(weights, axis=-1, keepdims=True))
    rounded = weights.astype(jnp.bfloat16)
    mixed = multiply('phmn,nphe->mphe', rounded, values.reshape(shape_four)).astype(jnp.bfloat16)
    return (weights, rounded, mixed.reshape(members, count, width))

def attend_back(query, keys, values, weights, rounded, upstream, heads):
    members, count, width = query.shape
    shape_four = (members, count, heads, width // heads)
    scale = 1.0 / math.sqrt(width // heads)
    up_four = upstream.reshape(shape_four)
    dprob = multiply('mphe,nphe->phmn', up_four, values.reshape(shape_four))
    grad_v = multiply('phmn,mphe->nphe', rounded, up_four).astype(jnp.bfloat16)
    dscore = (weights * (dprob - lax.optimization_barrier(jnp.sum(weights * dprob, axis=-1, keepdims=True))) * scale).astype(jnp.bfloat16)
    grad_q = multiply('phmn,nphe->mphe', dscore, keys.reshape(shape_four)).astype(jnp.bfloat16)
    grad_k = multiply('phmn,mphe->nphe', dscore, query.reshape(shape_four)).astype(jnp.bfloat16)
    return (grad_q.reshape(members, count, width), grad_k.reshape(members, count, width), grad_v.reshape(members, count, width))

def layer_block(inputs, cotangent, norm1_gain, w_query, w_key, w_value, w_out, norm2_gain, w_up, w_down):
    heads = inputs.shape[-1] // HEAD_DIM
    wide = inputs.astype(jnp.float32)
    unit1, inverse1 = norm_rows(wide)
    normed1 = (unit1 * norm1_gain).astype(jnp.bfloat16)
    query = multiply('mpd,de->mpe', normed1, w_query).astype(jnp.bfloat16)
    keys = multiply('mpd,de->mpe', normed1, w_key).astype(jnp.bfloat16)
    values = multiply('mpd,de->mpe', normed1, w_value).astype(jnp.bfloat16)
    weights, rounded, mixed = attend(query, keys, values, heads)
    hidden_state = wide + multiply('mpd,de->mpe', mixed, w_out)
    unit2, inverse2 = norm_rows(hidden_state)
    normed2 = (unit2 * norm2_gain).astype(jnp.bfloat16)
    preact = multiply('mpd,df->mpf', normed2, w_up)
    activated, slopes = gelu_pair(preact)
    activated = activated.astype(jnp.bfloat16)
    part_down = multiply('mpf,mpd->fd', activated, cotangent)
    grad_act = multiply('mpd,fd->mpf', cotangent, w_down)
    grad_pre = (grad_act * slopes).astype(jnp.bfloat16)
    part_up = multiply('mpd,mpf->df', normed2, grad_pre)
    grad_normed2 = multiply('mpf,df->mpd', grad_pre, w_up)
    back_two, part_gain2 = norm_back(unit2, inverse2, norm2_gain, grad_normed2)
    grad_hidden = cotangent.astype(jnp.float32) + back_two
    grad_attn = grad_hidden.astype(jnp.bfloat16)
    part_wout = multiply('mpd,mpe->de', mixed, grad_attn)
    grad_mixed = multiply('mpe,de->mpd', grad_attn, w_out).astype(jnp.bfloat16)
    grad_q, grad_k, grad_v = attend_back(query, keys, values, weights, rounded, grad_mixed, heads)
    part_query = multiply('mpd,mpe->de', normed1, grad_q)
    part_key = multiply('mpd,mpe->de', normed1, grad_k)
    part_value = multiply('mpd,mpe->de', normed1, grad_v)
    grad_normed1 = multiply('mpe,de->mpd', grad_q, w_query) + multiply('mpe,de->mpd', grad_k, w_key) + multiply('mpe,de->mpd', grad_v, w_value)
    back_one, part_gain1 = norm_back(unit1, inverse1, norm1_gain, grad_normed1)
    input_grad = grad_hidden + back_one
    return (input_grad, (part_query, part_key, part_value, part_wout, part_up, part_down, part_gain1, part_gain2))

def reference(layer_input, out_grad, norm1_gain, w_query, w_key, w_value, w_out, norm2_gain, w_up, w_down):
    block_size = math.gcd(PATCHES, 64)
    block_count = PATCHES // block_size

    def split_blocks(array):
        return array.reshape(MEMBERS, block_count, block_size, D).transpose(1, 0, 2, 3)
    square = jnp.zeros((D, D), jnp.float32)
    starting = (square, square, square, square, jnp.zeros((D, FF), jnp.float32), jnp.zeros((FF, D), jnp.float32), jnp.zeros((D,), jnp.float32), jnp.zeros((D,), jnp.float32))

    def advance(running, blocks):
        grad_in, parts = layer_block(blocks[0], blocks[1], norm1_gain, w_query, w_key, w_value, w_out, norm2_gain, w_up, w_down)
        return (tuple((first + second for first, second in zip(running, parts))), grad_in)
    totals, pieces = lax.scan(advance, starting, (split_blocks(layer_input), split_blocks(out_grad)))
    input_grad = pieces.transpose(1, 0, 2, 3).reshape(MEMBERS, PATCHES, D)
    scale = 1.0 / math.sqrt(MEMBERS * PATCHES)
    scaled = [part * scale for part in totals]
    return (input_grad, scaled[0], scaled[1], scaled[2], scaled[3], scaled[4], scaled[5], scaled[6], scaled[7])
```

```python
import functools
import math

import jax
import jax.numpy as jnp
from jax import lax
from jax.experimental import pallas as pl
from jax.experimental.pallas import tpu as pltpu
from jax.sharding import PartitionSpec as P

HEAD_DIM = 32
EPS = 1e-06
GELU_C = 0.7978845608028654
GELU_A = 0.044715
F32 = jnp.float32
BF16 = jnp.bfloat16


def dot(left, right):
    return lax.dot_general(left, right, (((1,), (0,)), ((), ())), preferred_element_type=F32)


def dot_nt(left, right):
    return lax.dot_general(left, right, (((1,), (1,)), ((), ())), preferred_element_type=F32)


def dot_tn(left, right):
    return lax.dot_general(left, right, (((0,), (0,)), ((), ())), preferred_element_type=F32)


def norm_rows(values):
    inverse = lax.rsqrt(jnp.mean(values * values, axis=-1, keepdims=True) + EPS)
    return values * inverse, inverse


def norm_back(unit_rows, inverse, gains, upstream):
    scaled = upstream * gains
    return inverse * (scaled - unit_rows * jnp.mean(scaled * unit_rows, axis=-1, keepdims=True))


def gelu_pair(preact):
    square = preact * preact
    tangent = jnp.tanh(GELU_C * (preact + GELU_A * preact * square))
    half = 0.5 * (1.0 + tangent)
    slopes = half + 0.5 * preact * (1.0 - tangent * tangent) * (
        GELU_C + (3.0 * GELU_A * GELU_C) * square
    )
    return preact * half, slopes


class Layer:
    def __init__(self, members, patches, width, hidden):
        self.members, self.patches, self.width, self.hidden = members, patches, width, hidden
        self.heads = width // HEAD_DIM
        self.groups, self.rows = patches // 8, members * 8
        self.tokens = self.groups * self.rows
        self.scale = 1.0 / math.sqrt(HEAD_DIM)

    def scratch(self):
        groups, rows, width, hidden = self.groups, self.rows, self.width, self.hidden
        return dict(
            x=pltpu.VMEM((groups, rows, width), F32),
            og=pltpu.VMEM((groups, rows, width), BF16),
            n1=pltpu.VMEM((groups, rows, width), BF16),
            q=pltpu.VMEM((groups, rows, width), BF16),
            k=pltpu.VMEM((groups, rows, width), BF16),
            v=pltpu.VMEM((groups, rows, width), BF16),
            mix=pltpu.VMEM((groups, rows, width), BF16),
            n2=pltpu.VMEM((groups, rows, width), BF16),
            act=pltpu.VMEM((groups, rows, hidden), BF16),
            pre=pltpu.VMEM((groups, rows, hidden), BF16),
            ga=pltpu.VMEM((groups, rows, width), BF16),
            gm=pltpu.VMEM((groups, rows, width), BF16),
            gh=pltpu.VMEM((groups, rows, width), F32),
            gq=pltpu.VMEM((groups, rows, width), BF16),
            gk=pltpu.VMEM((groups, rows, width), BF16),
            gv=pltpu.VMEM((groups, rows, width), BF16),
            p=pltpu.VMEM((groups, self.heads, rows, rows), F32),
        )

    def head_mask(self, head):
        lanes = lax.broadcasted_iota(jnp.int32, (1, self.width), 1)
        inside = (lanes >= head * HEAD_DIM) & (lanes < (head + 1) * HEAD_DIM)
        return jnp.where(inside, 1.0, 0.0).astype(BF16)

    def regroup(self, source, target):
        for pair in range(self.groups // 2):
            block = source[:, 16 * pair : 16 * pair + 16, :].astype(F32)
            for half in range(2):
                piece = block[:, 8 * half : 8 * half + 8, :].reshape(self.rows, self.width)
                target[2 * pair + half] = piece.astype(target.dtype)

    def ungroup(self, source, target):
        for pair in range(self.groups // 2):
            halves = [
                source[2 * pair + half].reshape(self.members, 8, self.width) for half in range(2)
            ]
            target[:, 16 * pair : 16 * pair + 16, :] = jnp.concatenate(halves, axis=1).astype(
                target.dtype
            )

    def attention(self, s, w, g):
        unit, _ = norm_rows(s["x"][g])
        normed = (unit * w["g1"][...]).astype(BF16)
        s["n1"][g] = normed
        query = dot(normed, w["wq"][...]).astype(BF16)
        keys = dot(normed, w["wk"][...]).astype(BF16)
        values = dot(normed, w["wv"][...]).astype(BF16)
        s["q"][g], s["k"][g], s["v"][g] = query, keys, values
        rows = self.rows
        same = (
            lax.broadcasted_iota(jnp.int32, (rows, rows), 0) % 8
            == lax.broadcasted_iota(jnp.int32, (rows, rows), 1) % 8
        )
        mixed = jnp.zeros((rows, self.width), F32)
        for head in range(self.heads):
            mask = self.head_mask(head)
            scores = jnp.where(same, dot_nt(query * mask, keys) * self.scale, -1e30)
            weights = jnp.exp(scores - jnp.max(scores, axis=-1, keepdims=True))
            weights = weights * (1.0 / jnp.sum(weights, axis=-1, keepdims=True))
            s["p"][g, head] = weights
            mixed += dot(weights.astype(BF16), values * mask)
        s["mix"][g] = mixed.astype(BF16)

    def feed_forward(self, s, w, g, gain2):
        mixed, out_grad = s["mix"][g], s["og"][g]
        state = s["x"][g] + dot(mixed, w["wo"][...])
        unit, inverse = norm_rows(state)
        normed = (unit * w["g2"][...]).astype(BF16)
        s["n2"][g] = normed
        grad_normed = jnp.zeros((self.rows, self.width), F32)
        step = 256
        for at in range(0, self.hidden, step):
            some = slice(at, at + step)
            activated, slopes = gelu_pair(dot(normed, w["wu"][:, some]))
            s["act"][g, :, some] = activated.astype(BF16)
            grad_pre = (dot_nt(out_grad, w["wd"][some, :]) * slopes).astype(BF16)
            s["pre"][g, :, some] = grad_pre
            grad_normed += dot_nt(grad_pre, w["wu"][:, some])
        grad_hidden = out_grad.astype(F32) + norm_back(unit, inverse, w["g2"][...], grad_normed)
        s["gh"][g] = grad_hidden
        grad_attn = grad_hidden.astype(BF16)
        s["ga"][g] = grad_attn
        s["gm"][g] = dot_nt(grad_attn, w["wo"][...]).astype(BF16)
        return gain2 + jnp.sum(grad_normed * unit, axis=0, keepdims=True)

    def attention_back(self, s, w, g, gain1):
        query, keys, values, upstream = s["q"][g], s["k"][g], s["v"][g], s["gm"][g]
        grad_q = jnp.zeros((self.rows, self.width), F32)
        grad_k, grad_v = grad_q, grad_q
        for head in range(self.heads):
            mask = self.head_mask(head)
            weights = s["p"][g, head]
            up = upstream * mask
            dprob = dot_nt(up, values)
            both = weights * dprob
            dscore = both - weights * jnp.sum(both, axis=-1, keepdims=True)
            dscore = (dscore * self.scale).astype(BF16)
            grad_v += dot_tn(weights.astype(BF16), up)
            grad_q += dot(dscore, keys * mask)
            grad_k += dot_tn(dscore, query * mask)
        grad_q, grad_k, grad_v = (grad.astype(BF16) for grad in (grad_q, grad_k, grad_v))
        s["gq"][g], s["gk"][g], s["gv"][g] = grad_q, grad_k, grad_v
        grad_normed = (
            dot_nt(grad_q, w["wq"][...])
            + dot_nt(grad_k, w["wk"][...])
            + dot_nt(grad_v, w["wv"][...])
        )
        unit, inverse = norm_rows(s["x"][g])
        back = norm_back(unit, inverse, w["g1"][...], grad_normed)
        s["gh"][g] = (s["gh"][g] - s["og"][g].astype(F32)) + back
        return gain1 + jnp.sum(grad_normed * unit, axis=0, keepdims=True)

    def flat(self, s, name):
        array = s[name][...]
        return array.reshape(self.tokens, array.shape[-1])

    def wide_parts(self, s, parts):
        out_grad, normed = self.flat(s, "og"), self.flat(s, "n2")
        for at in range(0, self.hidden, 256):
            some = slice(at, at + 256)
            act = s["act"][:, :, some].reshape(self.tokens, 256)
            parts[some, :] = dot_tn(act, out_grad)
            pre = s["pre"][:, :, some].reshape(self.tokens, 256)
            parts[self.hidden + at : self.hidden + at + 256, :] = dot_tn(normed, pre)

    def square_parts(self, s, parts):
        normed = self.flat(s, "n1")
        at = 2 * self.hidden
        for name in ("gq", "gk", "gv"):
            parts[at : at + self.width, :] = dot_tn(normed, self.flat(s, name))
            at += self.width
        parts[at : at + self.width, :] = dot_tn(self.flat(s, "mix"), self.flat(s, "ga"))


WEIGHTS = ("g1", "wq", "wk", "wv", "wo", "g2", "wu", "wd")


def kernel(layer, names, *refs):
    x_ref, og_ref = refs[:2]
    w = dict(zip(WEIGHTS, refs[2:10]))
    y_ref, parts_ref, gains_ref = refs[10:13]
    s = dict(zip(names, refs[13:]))
    layer.regroup(x_ref, s["x"])
    layer.regroup(og_ref, s["og"])
    zero = jnp.zeros((1, layer.width), F32)

    @pl.loop(0, layer.groups)
    def _(g):
        layer.attention(s, w, g)

    gain2 = lax.fori_loop(0, layer.groups, lambda g, c: layer.feed_forward(s, w, g, c), zero)
    layer.wide_parts(s, parts_ref)
    gain1 = lax.fori_loop(0, layer.groups, lambda g, c: layer.attention_back(s, w, g, c), zero)
    layer.square_parts(s, parts_ref)
    layer.ungroup(s["gh"], y_ref)
    gains_ref[0:1, :] = gain1
    gains_ref[1:2, :] = gain2


def on_device(x, og, g1, wq, wk, wv, wo, g2, wu, wd):
    groups = lax.axis_size("member")
    own_members, own_patches, width = x.shape
    spread = own_patches // groups
    everyone = own_members * groups
    hidden = wu.shape[1]
    layer = Layer(everyone, spread, width, hidden)

    def patchwise(array):
        array = array.reshape(own_members, groups, spread, width)
        array = lax.all_to_all(array, "member", split_axis=1, concat_axis=0, tiled=True)
        return array.reshape(everyone, spread, width)

    scratch = layer.scratch()
    vmem = pl.BlockSpec(memory_space=pltpu.VMEM)
    back, parts, gains = pl.pallas_call(
        functools.partial(kernel, layer, tuple(scratch)),
        out_shape=(
            jax.ShapeDtypeStruct((everyone, spread, width), BF16),
            jax.ShapeDtypeStruct((2 * hidden + 4 * width, width), F32),
            jax.ShapeDtypeStruct((2, width), F32),
        ),
        in_specs=[vmem] * 10,
        out_specs=(vmem, vmem, vmem),
        scratch_shapes=list(scratch.values()),
        compiler_params=pltpu.CompilerParams(vmem_limit_bytes=60 * 2**20),
    )(patchwise(x), patchwise(og), g1.reshape(1, width), wq, wk, wv, wo, g2.reshape(1, width), wu, wd)
    back = lax.all_to_all(
        back.reshape(everyone, 1, spread, width), "member", split_axis=0, concat_axis=1, tiled=True
    ).reshape(own_members, own_patches, width)
    input_grad = og.astype(F32) + back.astype(F32)
    scale = 1.0 / math.sqrt(everyone * own_patches * lax.axis_size("space"))
    parts, gains = lax.psum((parts, gains), ("member", "space"))
    return finish(input_grad, parts * scale, gains * scale, width, hidden)


def finish(input_grad, parts, gains, width, hidden):
    down = parts[:hidden]
    up = parts[hidden : 2 * hidden].reshape(hidden // width, width, width)
    up = up.transpose(1, 0, 2).reshape(width, hidden)
    squares = [parts[2 * hidden + width * i : 2 * hidden + width * (i + 1)] for i in range(4)]
    return (input_grad, *squares, up, down, gains[0], gains[1])


def solution(mesh):
    spread = P("member", "space", None)
    return jax.shard_map(
        on_device,
        mesh=mesh,
        in_specs=(spread, spread) + (P(),) * 8,
        out_specs=(spread,) + (P(),) * 8,
        check_vma=False,
    )
```

```python
import functools
import math

import jax
import jax.numpy as jnp
from jax import lax
from jax.experimental import pallas as pl
from jax.experimental.pallas import tpu as pltpu
from jax.sharding import PartitionSpec as P

HEAD_DIM = 32
EPS = 1e-06
GELU_C = 0.7978845608028654
GELU_A = 0.044715
F32 = jnp.float32
BF16 = jnp.bfloat16


def dot(left, right):
    return lax.dot_general(left, right, (((1,), (0,)), ((), ())), preferred_element_type=F32)


def dot_nt(left, right):
    return lax.dot_general(left, right, (((1,), (1,)), ((), ())), preferred_element_type=F32)


def dot_tn(left, right):
    return lax.dot_general(left, right, (((0,), (0,)), ((), ())), preferred_element_type=F32)


def norm_rows(values):
    inverse = lax.rsqrt(jnp.mean(values * values, axis=-1, keepdims=True) + EPS)
    return values * inverse, inverse


def norm_back(unit_rows, inverse, gains, upstream):
    scaled = upstream * gains
    return inverse * (scaled - unit_rows * jnp.mean(scaled * unit_rows, axis=-1, keepdims=True))


def gelu_pair(preact):
    square = preact * preact
    tangent = jnp.tanh(GELU_C * (preact + GELU_A * preact * square))
    half = 0.5 * (1.0 + tangent)
    slopes = half + 0.5 * preact * (1.0 - tangent * tangent) * (
        GELU_C + (3.0 * GELU_A * GELU_C) * square
    )
    return preact * half, slopes


class Layer:
    def __init__(self, members, patches, width, hidden):
        self.members, self.patches, self.width, self.hidden = members, patches, width, hidden
        self.heads = width // HEAD_DIM
        self.groups, self.rows = patches // 8, members * 8
        self.tokens = self.groups * self.rows
        self.scale = 1.0 / math.sqrt(HEAD_DIM)

    def scratch(self):
        groups, rows, width, hidden = self.groups, self.rows, self.width, self.hidden
        return dict(
            x=pltpu.VMEM((groups, rows, width), F32),
            og=pltpu.VMEM((groups, rows, width), BF16),
            n1=pltpu.VMEM((groups, rows, width), BF16),
            q=pltpu.VMEM((groups, rows, width), BF16),
            k=pltpu.VMEM((groups, rows, width), BF16),
            v=pltpu.VMEM((groups, rows, width), BF16),
            mix=pltpu.VMEM((groups, rows, width), BF16),
            n2=pltpu.VMEM((groups, rows, width), BF16),
            act=pltpu.VMEM((groups, rows, hidden), BF16),
            pre=pltpu.VMEM((groups, rows, hidden), BF16),
            ga=pltpu.VMEM((groups, rows, width), BF16),
            gm=pltpu.VMEM((groups, rows, width), BF16),
            gh=pltpu.VMEM((groups, rows, width), F32),
            gq=pltpu.VMEM((groups, rows, width), BF16),
            gk=pltpu.VMEM((groups, rows, width), BF16),
            gv=pltpu.VMEM((groups, rows, width), BF16),
            p=pltpu.VMEM((groups, self.heads, rows, rows), F32),
        )

    def head_mask(self, head):
        lanes = lax.broadcasted_iota(jnp.int32, (1, self.width), 1)
        inside = (lanes >= head * HEAD_DIM) & (lanes < (head + 1) * HEAD_DIM)
        return jnp.where(inside, 1.0, 0.0).astype(BF16)

    def regroup(self, source, target):
        for pair in range(self.groups // 2):
            block = source[:, 16 * pair : 16 * pair + 16, :].astype(F32)
            for half in range(2):
                piece = block[:, 8 * half : 8 * half + 8, :].reshape(self.rows, self.width)
                target[2 * pair + half] = piece.astype(target.dtype)

    def ungroup(self, source, target):
        for pair in range(self.groups // 2):
            halves = [
                source[2 * pair + half].reshape(self.members, 8, self.width) for half in range(2)
            ]
            target[:, 16 * pair : 16 * pair + 16, :] = jnp.concatenate(halves, axis=1).astype(
                target.dtype
            )

    def attention(self, s, w, g):
        unit, _ = norm_rows(s["x"][g])
        normed = (unit * w["g1"][...]).astype(BF16)
        s["n1"][g] = normed
        query = dot(normed, w["wq"][...]).astype(BF16)
        keys = dot(normed, w["wk"][...]).astype(BF16)
        values = dot(normed, w["wv"][...]).astype(BF16)
        s["q"][g], s["k"][g], s["v"][g] = query, keys, values
        rows = self.rows
        same = (
            lax.broadcasted_iota(jnp.int32, (rows, rows), 0) % 8
            == lax.broadcasted_iota(jnp.int32, (rows, rows), 1) % 8
        )
        mixed = jnp.zeros((rows, self.width), F32)
        for head in range(self.heads):
            mask = self.head_mask(head)
            scores = jnp.where(same, dot_nt(query * mask, keys) * self.scale, -1e30)
            weights = jnp.exp(scores - jnp.max(scores, axis=-1, keepdims=True))
            weights = weights * (1.0 / jnp.sum(weights, axis=-1, keepdims=True))
            s["p"][g, head] = weights
            mixed += dot(weights.astype(BF16), values * mask)
        s["mix"][g] = mixed.astype(BF16)

    def feed_forward(self, s, w, g, gain2):
        mixed, out_grad = s["mix"][g], s["og"][g]
        state = s["x"][g] + dot(mixed, w["wo"][...])
        unit, inverse = norm_rows(state)
        normed = (unit * w["g2"][...]).astype(BF16)
        s["n2"][g] = normed
        grad_normed = jnp.zeros((self.rows, self.width), F32)
        step = 256
        for at in range(0, self.hidden, step):
            some = slice(at, at + step)
            activated, slopes = gelu_pair(dot(normed, w["wu"][:, some]))
            s["act"][g, :, some] = activated.astype(BF16)
            grad_pre = (dot_nt(out_grad, w["wd"][some, :]) * slopes).astype(BF16)
            s["pre"][g, :, some] = grad_pre
            grad_normed += dot_nt(grad_pre, w["wu"][:, some])
        grad_hidden = out_grad.astype(F32) + norm_back(unit, inverse, w["g2"][...], grad_normed)
        s["gh"][g] = grad_hidden
        grad_attn = grad_hidden.astype(BF16)
        s["ga"][g] = grad_attn
        s["gm"][g] = dot_nt(grad_attn, w["wo"][...]).astype(BF16)
        return gain2 + jnp.sum(grad_normed * unit, axis=0, keepdims=True)

    def attention_back(self, s, w, g, gain1):
        query, keys, values, upstream = s["q"][g], s["k"][g], s["v"][g], s["gm"][g]
        grad_q = jnp.zeros((self.rows, self.width), F32)
        grad_k, grad_v = grad_q, grad_q
        for head in range(self.heads):
            mask = self.head_mask(head)
            weights = s["p"][g, head]
            up = upstream * mask
            dprob = dot_nt(up, values)
            both = weights * dprob
            dscore = both - weights * jnp.sum(both, axis=-1, keepdims=True)
            dscore = (dscore * self.scale).astype(BF16)
            grad_v += dot_tn(weights.astype(BF16), up)
            grad_q += dot(dscore, keys * mask)
            grad_k += dot_tn(dscore, query * mask)
        grad_q, grad_k, grad_v = (grad.astype(BF16) for grad in (grad_q, grad_k, grad_v))
        s["gq"][g], s["gk"][g], s["gv"][g] = grad_q, grad_k, grad_v
        grad_normed = (
            dot_nt(grad_q, w["wq"][...])
            + dot_nt(grad_k, w["wk"][...])
            + dot_nt(grad_v, w["wv"][...])
        )
        unit, inverse = norm_rows(s["x"][g])
        back = norm_back(unit, inverse, w["g1"][...], grad_normed)
        s["gh"][g] = (s["gh"][g] - s["og"][g].astype(F32)) + back
        return gain1 + jnp.sum(grad_normed * unit, axis=0, keepdims=True)

    def flat(self, s, name):
        array = s[name][...]
        return array.reshape(self.tokens, array.shape[-1])

    def wide_parts(self, s, parts):
        out_grad, normed = self.flat(s, "og"), self.flat(s, "n2")
        for at in range(0, self.hidden, 256):
            some = slice(at, at + 256)
            act = s["act"][:, :, some].reshape(self.tokens, 256)
            parts[some, :] = dot_tn(act, out_grad)
            pre = s["pre"][:, :, some].reshape(self.tokens, 256)
            parts[self.hidden + at : self.hidden + at + 256, :] = dot_tn(normed, pre)
        self.clear_rest(parts, 2 * self.hidden)

    def square_parts(self, s, parts):
        normed = self.flat(s, "n1")
        at = 0
        for name in ("gq", "gk", "gv"):
            parts[at : at + self.width, :] = dot_tn(normed, self.flat(s, name))
            at += self.width
        parts[at : at + self.width, :] = dot_tn(self.flat(s, "mix"), self.flat(s, "ga"))
        self.clear_rest(parts, at + self.width)

    def clear_rest(self, parts, used):
        rest = parts.shape[0] - used
        if rest:
            parts[used:, :] = jnp.zeros((rest, self.width), F32)


WEIGHTS = ("g1", "wq", "wk", "wv", "wo", "g2", "wu", "wd")


def kernel(layer, names, *refs):
    x_ref, og_ref = refs[:2]
    w = dict(zip(WEIGHTS, refs[2:10]))
    y_ref, wide_ref, square_ref, gains_ref = refs[10:14]
    s = dict(zip(names, refs[14:]))
    layer.regroup(x_ref, s["x"])
    layer.regroup(og_ref, s["og"])
    zero = jnp.zeros((1, layer.width), F32)

    @pl.loop(0, layer.groups)
    def _(g):
        layer.attention(s, w, g)

    gain2 = lax.fori_loop(0, layer.groups, lambda g, c: layer.feed_forward(s, w, g, c), zero)
    layer.wide_parts(s, wide_ref)
    gain1 = lax.fori_loop(0, layer.groups, lambda g, c: layer.attention_back(s, w, g, c), zero)
    layer.square_parts(s, square_ref)
    layer.ungroup(s["gh"], y_ref)
    gains_ref[...] = jnp.zeros_like(gains_ref)
    gains_ref[0:1, :] = gain1
    gains_ref[1:2, :] = gain2


class Ring:
    def __init__(self):
        self.member, self.space = lax.axis_index("member"), lax.axis_index("space")
        self.members, self.spaces = lax.axis_size("member"), lax.axis_size("space")
        self.chips = self.members // 2
        self.core = lax.rem(self.member, 2)
        self.chip = self.member // 2

    def member_peer(self, off):
        return lax.rem(self.member + off, self.members)

    def sibling(self):
        return self.member + 1 - 2 * self.core

    def chip_peer(self, off):
        return lax.rem(self.chip + off, self.chips)

    def space_peer(self, off):
        return lax.rem(self.space + off, self.spaces)

    def barrier(self, along_space):
        barrier = pltpu.get_barrier_semaphore()
        targets = [(self.member_peer(off), self.space) for off in range(1, self.members)]
        if along_space:
            targets += [(self.member, self.space_peer(off)) for off in range(1, self.spaces)]
        for target in targets:
            pl.semaphore_signal(
                barrier, inc=1, device_id=target, device_id_type=pl.DeviceIdType.MESH
            )
        pl.semaphore_wait(barrier, len(targets))


def send(source, target, sems, slot, device):
    copy = pltpu.make_async_remote_copy(
        src_ref=source,
        dst_ref=target,
        send_sem=sems.at[0, slot],
        recv_sem=sems.at[1, slot],
        device_id=device,
        device_id_type=pl.DeviceIdType.MESH,
    )
    copy.start()
    return copy


def some_rows(start, size):
    return pl.ds(pl.multiple_of(start, 16), size)


class Exchange:
    def __init__(self, ring, own, spread):
        self.ring, self.own, self.spread = ring, own, spread

    def mine(self, ref, index):
        return ref.at[:, some_rows(index * self.spread, self.spread), :]

    def here(self, ref, index):
        return ref.at[pl.ds(index * self.own, self.own), :, :]

    def start(self, source, target, sems, local, to_patch):
        ring = self.ring
        take, put = (self.mine, self.here) if to_patch else (self.here, self.mine)
        self.copies = []
        for off in range(1, ring.members):
            peer = ring.member_peer(off)
            self.copies.append(
                send(take(source, peer), put(target, ring.member), sems, off, (peer, ring.space))
            )
        own = pltpu.make_async_copy(take(source, ring.member), put(target, ring.member), local)
        own.start()
        self.copies.append(own)
        return self

    def wait(self):
        for copy in self.copies:
            copy.wait()


class Total:
    def __init__(self, ring, scale, parts, full, recv_a, send_b, recv_b, send_c, recv_c, own, sems):
        self.ring, self.scale = ring, scale
        self.parts, self.full, self.sems, self.own = parts, full, sems, own
        self.recv_a, self.send_b, self.recv_b = recv_a, send_b, recv_b
        self.send_c, self.recv_c = send_c, recv_c
        self.rows_a = parts.shape[0] // 2
        self.rows_b = self.rows_a // ring.chips
        self.rows_c = self.rows_b // ring.spaces
        self.at_a = ring.core * self.rows_a
        self.at_b = self.at_a + ring.chip * self.rows_b
        self.at_c = self.at_b + ring.space * self.rows_c

    @staticmethod
    def scratch(rows, width, chips, spaces):
        a = rows // 2
        b = a // chips
        c = b // spaces
        slots = 2 * (chips + spaces)
        return [
            pltpu.VMEM((rows, width), BF16),
            pltpu.VMEM((a, width), F32),
            pltpu.VMEM((a, width), BF16),
            pltpu.VMEM((chips, b, width), BF16),
            pltpu.VMEM((b, width), BF16),
            pltpu.VMEM((spaces, c, width), BF16),
            pltpu.VMEM((b, width), F32),
            pltpu.SemaphoreType.DMA((2, slots)),
        ]

    def start(self):
        ring = self.ring
        other = some_rows((1 - ring.core) * self.rows_a, self.rows_a)
        self.copies = [
            send(self.parts.at[other], self.recv_a, self.sems, 0, (ring.sibling(), ring.space))
        ]

    def wait(self):
        for copy in self.copies:
            copy.wait()

    def to_chips(self):
        ring = self.ring
        self.wait()
        self.copies = []
        for off in range(1, ring.chips):
            peer = ring.chip_peer(off)
            at = peer * self.rows_b
            rows = some_rows(at, self.rows_b)
            term = self.parts[some_rows(self.at_a + at, self.rows_b), :] + self.recv_a[rows, :]
            self.send_b[rows, :] = term.astype(BF16)
            device = (2 * peer + ring.core, ring.space)
            self.copies.append(
                send(self.send_b.at[rows], self.recv_b.at[off], self.sems, off, device)
            )
        mine = some_rows(ring.chip * self.rows_b, self.rows_b)
        self.own[...] = self.parts[some_rows(self.at_b, self.rows_b), :] + self.recv_a[mine, :]

    def to_spaces(self):
        ring = self.ring
        self.wait()
        self.copies = []
        total = self.own[...]
        for off in range(1, ring.chips):
            total += self.recv_b[off].astype(F32)
        self.own[...] = total
        self.send_c[...] = total.astype(BF16)
        for off in range(1, ring.spaces):
            peer = ring.space_peer(off)
            rows = some_rows(peer * self.rows_c, self.rows_c)
            slot = ring.chips + off
            self.copies.append(
                send(self.send_c.at[rows], self.recv_c.at[off], self.sems, slot, (ring.member, peer))
            )

    def gather_spaces(self):
        ring = self.ring
        self.wait()
        total = self.own[some_rows(ring.space * self.rows_c, self.rows_c), :]
        for off in range(1, ring.spaces):
            total += self.recv_c[off].astype(F32)
        rows = some_rows(self.at_c, self.rows_c)
        self.full[rows, :] = (total * self.scale).astype(BF16)
        place = self.full.at[rows]
        base = ring.chips + ring.spaces
        self.copies = [
            send(place, place, self.sems, base + off, (ring.member, ring.space_peer(off)))
            for off in range(1, ring.spaces)
        ]

    def gather_chips(self):
        ring = self.ring
        self.wait()
        place = self.full.at[some_rows(self.at_b, self.rows_b)]
        base = ring.chips + 2 * ring.spaces
        self.copies = [
            send(
                place, place, self.sems, base + off, (2 * ring.chip_peer(off) + ring.core, ring.space)
            )
            for off in range(1, ring.chips)
        ]

    def gather_cores(self):
        ring = self.ring
        self.wait()
        place = self.full.at[some_rows(self.at_a, self.rows_a)]
        slot = ring.chips + 2 * ring.spaces
        self.copies = [send(place, place, self.sems, slot, (ring.sibling(), ring.space))]


class Gains:
    def __init__(self, ring, value, recv, sems):
        self.ring, self.value, self.recv, self.sems = ring, value, recv, sems

    @staticmethod
    def scratch(width, chips, spaces):
        return [
            pltpu.VMEM((3, 8, width), F32),
            pltpu.VMEM((chips + spaces, 8, width), F32),
            pltpu.SemaphoreType.DMA((2, chips + spaces)),
        ]

    def peers(self, stage):
        ring = self.ring
        if stage == 0:
            return [(0, (ring.sibling(), ring.space))]
        if stage == 1:
            return [
                (off, (2 * ring.chip_peer(off) + ring.core, ring.space))
                for off in range(1, ring.chips)
            ]
        return [
            (ring.chips + off, (ring.member, ring.space_peer(off)))
            for off in range(1, ring.spaces)
        ]

    def start(self, stage):
        self.copies = [
            send(self.value.at[stage], self.recv.at[slot], self.sems, slot, device)
            for slot, device in self.peers(stage)
        ]

    def finish(self, stage):
        for copy in self.copies:
            copy.wait()
        total = self.value[stage]
        for slot, _ in self.peers(stage):
            total += self.recv[slot]
        return total


def fetch_kernel(x_ref, og_ref, x_out, og_out, x_sems, og_sems, local):
    ring = Ring()
    ring.barrier(False)
    moves = []
    for i, (source, target, sems) in enumerate(
        ((x_ref, x_out, x_sems), (og_ref, og_out, og_sems))
    ):
        move = Exchange(ring, source.shape[0], target.shape[1])
        moves.append(move.start(source, target, sems, local.at[i], True))
    for move in moves:
        move.wait()


def reduce_all(ring, pieces, gains, gains_ref, scale):
    for piece in pieces:
        piece.start()
    gains.start(0)
    for piece in pieces:
        piece.to_chips()
    gains.value[1] = gains.finish(0)
    gains.start(1)
    for piece in pieces:
        piece.to_spaces()
    gains.value[2] = gains.finish(1)
    gains.start(2)
    for piece in pieces:
        piece.gather_spaces()
    for piece in pieces:
        piece.gather_chips()
    for piece in pieces:
        piece.gather_cores()
    gains_ref[...] = gains.finish(2) * scale
    for piece in pieces:
        piece.wait()


def share_kernel(scale, back_ref, wide_ref, square_ref, gain_ref, y_ref, wide_out, square_out,
                 gains_out, *scratch):
    ring = Ring()
    ring.barrier(True)
    y_sems, local = scratch[:2]
    move = Exchange(ring, y_ref.shape[0], back_ref.shape[1])
    pieces = [
        Total(ring, scale, wide_ref, wide_out, *scratch[2:9]),
        Total(ring, scale, square_ref, square_out, *scratch[9:16]),
    ]
    gains = Gains(ring, *scratch[16:19])
    gains.value[0] = gain_ref[...]
    move.start(back_ref, y_ref, y_sems, local.at[0], False)
    reduce_all(ring, pieces, gains, gains_out, scale)
    move.wait()


def padded(rows, devices):
    unit = 16 * devices
    return -(-rows // unit) * unit


def on_device(x, og, g1, wq, wk, wv, wo, g2, wu, wd):
    groups, spaces = lax.axis_size("member"), lax.axis_size("space")
    own_members, own_patches, width = x.shape
    spread = own_patches // groups
    everyone = own_members * groups
    hidden = wu.shape[1]
    layer = Layer(everyone, spread, width, hidden)
    vmem = pl.BlockSpec(memory_space=pltpu.VMEM)
    limit = 60 * 2**20
    moved = jax.ShapeDtypeStruct((everyone, spread, width), BF16)
    x_here, og_here = pl.pallas_call(
        fetch_kernel,
        out_shape=(moved, moved),
        in_specs=[vmem] * 2,
        out_specs=(vmem, vmem),
        scratch_shapes=[
            pltpu.SemaphoreType.DMA((2, groups)),
            pltpu.SemaphoreType.DMA((2, groups)),
            pltpu.SemaphoreType.DMA((2,)),
        ],
        compiler_params=pltpu.CompilerParams(
            vmem_limit_bytes=limit, collective_id=0, has_side_effects=True
        ),
    )(x, og)
    wide_rows = padded(2 * hidden, groups * spaces)
    square_rows = padded(4 * width, groups * spaces)
    scratch = layer.scratch()
    back, wide, square, gains = pl.pallas_call(
        functools.partial(kernel, layer, tuple(scratch)),
        out_shape=(
            moved,
            jax.ShapeDtypeStruct((wide_rows, width), F32),
            jax.ShapeDtypeStruct((square_rows, width), F32),
            jax.ShapeDtypeStruct((8, width), F32),
        ),
        in_specs=[vmem] * 10,
        out_specs=(vmem,) * 4,
        scratch_shapes=list(scratch.values()),
        compiler_params=pltpu.CompilerParams(vmem_limit_bytes=limit),
    )(x_here, og_here, g1.reshape(1, width), wq, wk, wv, wo, g2.reshape(1, width), wu, wd)
    scale = 1.0 / math.sqrt(everyone * own_patches * spaces)
    chips = groups // 2
    back, wide, square, gains = pl.pallas_call(
        functools.partial(share_kernel, scale),
        out_shape=(
            jax.ShapeDtypeStruct(x.shape, BF16),
            jax.ShapeDtypeStruct((wide_rows, width), BF16),
            jax.ShapeDtypeStruct((square_rows, width), BF16),
            jax.ShapeDtypeStruct((8, width), F32),
        ),
        in_specs=[vmem] * 4,
        out_specs=(vmem,) * 4,
        scratch_shapes=[
            pltpu.SemaphoreType.DMA((2, groups)),
            pltpu.SemaphoreType.DMA((1,)),
            *Total.scratch(wide_rows, width, chips, spaces)[1:],
            *Total.scratch(square_rows, width, chips, spaces)[1:],
            *Gains.scratch(width, chips, spaces),
        ],
        compiler_params=pltpu.CompilerParams(
            vmem_limit_bytes=limit, collective_id=1, has_side_effects=True
        ),
    )(back, wide, square, gains)
    return finish(og, back, wide, square, gains, width, hidden)


def finish(og, back, wide, square, gains, width, hidden):
    input_grad = og.astype(F32) + back.astype(F32)
    wide, square = wide.astype(F32), square.astype(F32)
    up = wide[hidden : 2 * hidden].reshape(hidden // width, width, width)
    up = up.transpose(1, 0, 2).reshape(width, hidden)
    squares = [square[width * i : width * (i + 1)] for i in range(4)]
    return (input_grad, *squares, up, wide[:hidden], gains[0], gains[1])


def solution(mesh):
    spread = P("member", "space", None)
    return jax.shard_map(
        on_device,
        mesh=mesh,
        in_specs=(spread, spread) + (P(),) * 8,
        out_specs=(spread,) + (P(),) * 8,
        check_vma=False,
    )
```

```python
import functools
import math

import jax
import jax.numpy as jnp
from jax import lax
from jax.experimental import pallas as pl
from jax.experimental.pallas import tpu as pltpu
from jax.sharding import PartitionSpec as P

HEAD_DIM = 32
EPS = 1e-06
GELU_C = 0.7978845608028654
GELU_A = 0.044715
F32 = jnp.float32
BF16 = jnp.bfloat16


def dot(left, right):
    return lax.dot_general(left, right, (((1,), (0,)), ((), ())), preferred_element_type=F32)


def dot_nt(left, right):
    return lax.dot_general(left, right, (((1,), (1,)), ((), ())), preferred_element_type=F32)


def dot_tn(left, right):
    return lax.dot_general(left, right, (((0,), (0,)), ((), ())), preferred_element_type=F32)


def norm_rows(values):
    inverse = lax.rsqrt(jnp.mean(values * values, axis=-1, keepdims=True) + EPS)
    return values * inverse, inverse


def norm_back(unit_rows, inverse, gains, upstream):
    scaled = upstream * gains
    return inverse * (scaled - unit_rows * jnp.mean(scaled * unit_rows, axis=-1, keepdims=True))


def gelu_pair(preact):
    square = preact * preact
    tangent = jnp.tanh(GELU_C * (preact + GELU_A * preact * square))
    half = 0.5 * (1.0 + tangent)
    slopes = half + 0.5 * preact * (1.0 - tangent * tangent) * (
        GELU_C + (3.0 * GELU_A * GELU_C) * square
    )
    return preact * half, slopes


class Layer:
    def __init__(self, members, patches, width, hidden):
        self.members, self.patches, self.width, self.hidden = members, patches, width, hidden
        self.heads = width // HEAD_DIM
        self.groups, self.rows = patches // 8, members * 8
        self.tokens = self.groups * self.rows
        self.scale = 1.0 / math.sqrt(HEAD_DIM)

    def scratch(self):
        groups, rows, width, hidden = self.groups, self.rows, self.width, self.hidden
        return dict(
            x=pltpu.VMEM((groups, rows, width), F32),
            og=pltpu.VMEM((groups, rows, width), BF16),
            n1=pltpu.VMEM((groups, rows, width), BF16),
            q=pltpu.VMEM((groups, rows, width), BF16),
            k=pltpu.VMEM((groups, rows, width), BF16),
            v=pltpu.VMEM((groups, rows, width), BF16),
            mix=pltpu.VMEM((groups, rows, width), BF16),
            n2=pltpu.VMEM((groups, rows, width), BF16),
            act=pltpu.VMEM((groups, rows, hidden), BF16),
            pre=pltpu.VMEM((groups, rows, hidden), BF16),
            ga=pltpu.VMEM((groups, rows, width), BF16),
            gm=pltpu.VMEM((groups, rows, width), BF16),
            gh=pltpu.VMEM((groups, rows, width), F32),
            p=pltpu.VMEM((groups, self.heads, rows, rows), F32),
        )

    def head_mask(self, head):
        lanes = lax.broadcasted_iota(jnp.int32, (1, self.width), 1)
        inside = (lanes >= head * HEAD_DIM) & (lanes < (head + 1) * HEAD_DIM)
        return jnp.where(inside, 1.0, 0.0).astype(BF16)

    def regroup(self, source, target):
        for pair in range(self.groups // 2):
            block = source[:, 16 * pair : 16 * pair + 16, :].astype(F32)
            for half in range(2):
                piece = block[:, 8 * half : 8 * half + 8, :].reshape(self.rows, self.width)
                target[2 * pair + half] = piece.astype(target.dtype)

    def ungroup(self, source, target):
        for pair in range(self.groups // 2):
            halves = [
                source[2 * pair + half].reshape(self.members, 8, self.width) for half in range(2)
            ]
            target[:, 16 * pair : 16 * pair + 16, :] = jnp.concatenate(halves, axis=1).astype(
                target.dtype
            )

    def attention(self, s, w, g):
        unit, _ = norm_rows(s["x"][g])
        normed = (unit * w["g1"][...]).astype(BF16)
        s["n1"][g] = normed
        query = dot(normed, w["wq"][...]).astype(BF16)
        keys = dot(normed, w["wk"][...]).astype(BF16)
        values = dot(normed, w["wv"][...]).astype(BF16)
        s["q"][g], s["k"][g], s["v"][g] = query, keys, values
        rows = self.rows
        same = (
            lax.broadcasted_iota(jnp.int32, (rows, rows), 0) % 8
            == lax.broadcasted_iota(jnp.int32, (rows, rows), 1) % 8
        )
        mixed = jnp.zeros((rows, self.width), F32)
        for head in range(self.heads):
            mask = self.head_mask(head)
            scores = jnp.where(same, dot_nt(query * mask, keys) * self.scale, -1e30)
            weights = jnp.exp(scores - jnp.max(scores, axis=-1, keepdims=True))
            weights = weights * (1.0 / jnp.sum(weights, axis=-1, keepdims=True))
            s["p"][g, head] = weights
            mixed += dot(weights.astype(BF16), values * mask)
        s["mix"][g] = mixed.astype(BF16)

    def feed_forward(self, s, w, g, gain2):
        mixed, out_grad = s["mix"][g], s["og"][g]
        state = s["x"][g] + dot(mixed, w["wo"][...])
        unit, inverse = norm_rows(state)
        normed = (unit * w["g2"][...]).astype(BF16)
        s["n2"][g] = normed
        grad_normed = jnp.zeros((self.rows, self.width), F32)
        step = 256
        for at in range(0, self.hidden, step):
            some = slice(at, at + step)
            activated, slopes = gelu_pair(dot(normed, w["wu"][:, some]))
            s["act"][g, :, some] = activated.astype(BF16)
            grad_pre = (dot_nt(out_grad, w["wd"][some, :]) * slopes).astype(BF16)
            s["pre"][g, :, some] = grad_pre
            grad_normed += dot_nt(grad_pre, w["wu"][:, some])
        grad_hidden = out_grad.astype(F32) + norm_back(unit, inverse, w["g2"][...], grad_normed)
        s["gh"][g] = grad_hidden
        grad_attn = grad_hidden.astype(BF16)
        s["ga"][g] = grad_attn
        s["gm"][g] = dot_nt(grad_attn, w["wo"][...]).astype(BF16)
        return gain2 + jnp.sum(grad_normed * unit, axis=0, keepdims=True)

    def attention_back(self, s, w, g, gain1):
        query, keys, values, upstream = s["q"][g], s["k"][g], s["v"][g], s["gm"][g]
        grad_q = jnp.zeros((self.rows, self.width), F32)
        grad_k, grad_v = grad_q, grad_q
        for head in range(self.heads):
            mask = self.head_mask(head)
            weights = s["p"][g, head]
            up = upstream * mask
            dprob = dot_nt(up, values)
            both = weights * dprob
            dscore = both - weights * jnp.sum(both, axis=-1, keepdims=True)
            dscore = (dscore * self.scale).astype(BF16)
            grad_v += dot_tn(weights.astype(BF16), up)
            grad_q += dot(dscore, keys * mask)
            grad_k += dot_tn(dscore, query * mask)
        grad_q, grad_k, grad_v = (grad.astype(BF16) for grad in (grad_q, grad_k, grad_v))
        s["q"][g], s["k"][g], s["v"][g] = grad_q, grad_k, grad_v
        grad_normed = (
            dot_nt(grad_q, w["wq"][...])
            + dot_nt(grad_k, w["wk"][...])
            + dot_nt(grad_v, w["wv"][...])
        )
        unit, inverse = norm_rows(s["x"][g])
        back = norm_back(unit, inverse, w["g1"][...], grad_normed)
        s["gh"][g] = (s["gh"][g] - s["og"][g].astype(F32)) + back
        return gain1 + jnp.sum(grad_normed * unit, axis=0, keepdims=True)

    def flat(self, s, name):
        array = s[name][...]
        return array.reshape(self.tokens, array.shape[-1])

    def wide_parts(self, s, parts):
        out_grad, normed = self.flat(s, "og"), self.flat(s, "n2")
        for at in range(0, self.hidden, 256):
            some = slice(at, at + 256)
            act = s["act"][:, :, some].reshape(self.tokens, 256)
            parts[some, :] = dot_tn(act, out_grad)
            pre = s["pre"][:, :, some].reshape(self.tokens, 256)
            parts[self.hidden + at : self.hidden + at + 256, :] = dot_tn(normed, pre)
        self.clear_rest(parts, 2 * self.hidden)

    def square_parts(self, s, parts):
        normed = self.flat(s, "n1")
        at = 0
        for name in ("q", "k", "v"):
            parts[at : at + self.width, :] = dot_tn(normed, self.flat(s, name))
            at += self.width
        parts[at : at + self.width, :] = dot_tn(self.flat(s, "mix"), self.flat(s, "ga"))
        self.clear_rest(parts, at + self.width)

    def clear_rest(self, parts, used):
        rest = parts.shape[0] - used
        if rest:
            parts[used:, :] = jnp.zeros((rest, self.width), F32)


WEIGHTS = ("g1", "wq", "wk", "wv", "wo", "g2", "wu", "wd")


class Ring:
    def __init__(self):
        self.member, self.space = lax.axis_index("member"), lax.axis_index("space")
        self.members, self.spaces = lax.axis_size("member"), lax.axis_size("space")
        self.chips = self.members // 2
        self.core = lax.rem(self.member, 2)
        self.chip = self.member // 2

    def member_peer(self, off):
        return lax.rem(self.member + off, self.members)

    def sibling(self):
        return self.member + 1 - 2 * self.core

    def chip_peer(self, off):
        return lax.rem(self.chip + off, self.chips)

    def space_peer(self, off):
        return lax.rem(self.space + off, self.spaces)

    def barrier(self, along_space):
        barrier = pltpu.get_barrier_semaphore()
        targets = [(self.member_peer(off), self.space) for off in range(1, self.members)]
        if along_space:
            targets += [(self.member, self.space_peer(off)) for off in range(1, self.spaces)]
        for target in targets:
            pl.semaphore_signal(
                barrier, inc=1, device_id=target, device_id_type=pl.DeviceIdType.MESH
            )
        pl.semaphore_wait(barrier, len(targets))


def send(source, target, sems, slot, device):
    copy = pltpu.make_async_remote_copy(
        src_ref=source,
        dst_ref=target,
        send_sem=sems.at[0, slot],
        recv_sem=sems.at[1, slot],
        device_id=device,
        device_id_type=pl.DeviceIdType.MESH,
    )
    copy.start()
    return copy


def some_rows(start, size):
    return pl.ds(pl.multiple_of(start, 16), size)


class Exchange:
    def __init__(self, ring, own, spread):
        self.ring, self.own, self.spread = ring, own, spread

    def mine(self, ref, index):
        return ref.at[:, some_rows(index * self.spread, self.spread), :]

    def here(self, ref, index):
        return ref.at[pl.ds(index * self.own, self.own), :, :]

    def start(self, source, target, sems, local, to_patch):
        ring = self.ring
        take, put = (self.mine, self.here) if to_patch else (self.here, self.mine)
        self.copies = []
        for off in range(1, ring.members):
            peer = ring.member_peer(off)
            self.copies.append(
                send(take(source, peer), put(target, ring.member), sems, off, (peer, ring.space))
            )
        own = pltpu.make_async_copy(take(source, ring.member), put(target, ring.member), local)
        own.start()
        self.copies.append(own)
        return self

    def wait(self):
        for copy in self.copies:
            copy.wait()


class Total:
    def __init__(self, ring, scale, parts, full, recv_a, send_b, recv_b, send_c, recv_c, own, sems):
        self.ring, self.scale = ring, scale
        self.parts, self.full, self.sems, self.own = parts, full, sems, own
        self.recv_a, self.send_b, self.recv_b = recv_a, send_b, recv_b
        self.send_c, self.recv_c = send_c, recv_c
        self.rows_a = parts.shape[0] // 2
        self.rows_b = self.rows_a // ring.chips
        self.rows_c = self.rows_b // ring.spaces
        self.at_a = ring.core * self.rows_a
        self.at_b = self.at_a + ring.chip * self.rows_b
        self.at_c = self.at_b + ring.space * self.rows_c

    @staticmethod
    def scratch(rows, width, chips, spaces, held):
        a = rows // 2
        b = a // chips
        c = b // spaces
        slots = 2 * (chips + spaces)
        return [
            pltpu.VMEM((a, width), F32),
            pltpu.VMEM((a, width), held),
            pltpu.VMEM((chips, b, width), held),
            pltpu.VMEM((b, width), held),
            pltpu.VMEM((spaces, c, width), held),
            pltpu.VMEM((b, width), F32),
            pltpu.SemaphoreType.DMA((2, slots)),
        ]

    def start(self):
        ring = self.ring
        other = some_rows((1 - ring.core) * self.rows_a, self.rows_a)
        self.copies = [
            send(self.parts.at[other], self.recv_a, self.sems, 0, (ring.sibling(), ring.space))
        ]

    def wait(self):
        for copy in self.copies:
            copy.wait()

    def to_chips(self):
        ring = self.ring
        self.wait()
        self.copies = []
        for off in range(1, ring.chips):
            peer = ring.chip_peer(off)
            at = peer * self.rows_b
            rows = some_rows(at, self.rows_b)
            term = self.parts[some_rows(self.at_a + at, self.rows_b), :] + self.recv_a[rows, :]
            self.send_b[rows, :] = term.astype(self.send_b.dtype)
            device = (2 * peer + ring.core, ring.space)
            self.copies.append(
                send(self.send_b.at[rows], self.recv_b.at[off], self.sems, off, device)
            )
        mine = some_rows(ring.chip * self.rows_b, self.rows_b)
        self.own[...] = self.parts[some_rows(self.at_b, self.rows_b), :] + self.recv_a[mine, :]

    def to_spaces(self):
        ring = self.ring
        self.wait()
        self.copies = []
        total = self.own[...]
        for off in range(1, ring.chips):
            total += self.recv_b[off].astype(F32)
        self.own[...] = total
        self.send_c[...] = total.astype(self.send_c.dtype)
        for off in range(1, ring.spaces):
            peer = ring.space_peer(off)
            rows = some_rows(peer * self.rows_c, self.rows_c)
            slot = ring.chips + off
            self.copies.append(
                send(self.send_c.at[rows], self.recv_c.at[off], self.sems, slot, (ring.member, peer))
            )

    def gather_spaces(self):
        ring = self.ring
        self.wait()
        total = self.own[some_rows(ring.space * self.rows_c, self.rows_c), :]
        for off in range(1, ring.spaces):
            total += self.recv_c[off].astype(F32)
        rows = some_rows(self.at_c, self.rows_c)
        self.full[rows, :] = (total * self.scale).astype(BF16)
        place = self.full.at[rows]
        base = ring.chips + ring.spaces
        self.copies = [
            send(place, place, self.sems, base + off, (ring.member, ring.space_peer(off)))
            for off in range(1, ring.spaces)
        ]

    def gather_chips(self):
        ring = self.ring
        self.wait()
        place = self.full.at[some_rows(self.at_b, self.rows_b)]
        base = ring.chips + 2 * ring.spaces
        self.copies = [
            send(
                place, place, self.sems, base + off, (2 * ring.chip_peer(off) + ring.core, ring.space)
            )
            for off in range(1, ring.chips)
        ]

    def gather_cores(self):
        ring = self.ring
        self.wait()
        place = self.full.at[some_rows(self.at_a, self.rows_a)]
        slot = ring.chips + 2 * ring.spaces
        self.copies = [send(place, place, self.sems, slot, (ring.sibling(), ring.space))]


class Gains:
    def __init__(self, ring, value, recv, sems):
        self.ring, self.value, self.recv, self.sems = ring, value, recv, sems

    @staticmethod
    def scratch(width, chips, spaces):
        return [
            pltpu.VMEM((3, 8, width), F32),
            pltpu.VMEM((chips + spaces, 8, width), F32),
            pltpu.SemaphoreType.DMA((2, chips + spaces)),
        ]

    def peers(self, stage):
        ring = self.ring
        if stage == 0:
            return [(0, (ring.sibling(), ring.space))]
        if stage == 1:
            return [
                (off, (2 * ring.chip_peer(off) + ring.core, ring.space))
                for off in range(1, ring.chips)
            ]
        return [
            (ring.chips + off, (ring.member, ring.space_peer(off)))
            for off in range(1, ring.spaces)
        ]

    def start(self, stage):
        self.copies = [
            send(self.value.at[stage], self.recv.at[slot], self.sems, slot, device)
            for slot, device in self.peers(stage)
        ]

    def finish(self, stage):
        for copy in self.copies:
            copy.wait()
        total = self.value[stage]
        for slot, _ in self.peers(stage):
            total += self.recv[slot]
        return total


def kernel(layer, scale, names, *refs):
    x_ref, og_ref = refs[:2]
    w = dict(zip(WEIGHTS, refs[2:10]))
    y_ref, wide_out, square_out, gains_out = refs[10:14]
    s = dict(zip(names, refs[14:]))
    rest = refs[14 + len(names) :]
    x_here, og_here, x_sems, og_sems, y_sems, local, wide_ref, square_ref = rest[:8]
    ring = Ring()
    wide = Total(ring, scale, wide_ref, wide_out, *rest[8:15])
    square = Total(ring, scale, square_ref, square_out, *rest[15:22])
    gains = Gains(ring, *rest[22:25])
    own, spread = x_ref.shape[0], layer.patches
    x_move, og_move, y_move = (Exchange(ring, own, spread) for _ in range(3))

    ring.barrier(True)
    x_move.start(x_ref, x_here, x_sems, local.at[0], True)
    og_move.start(og_ref, og_here, og_sems, local.at[1], True)
    x_move.wait()
    layer.regroup(x_here, s["x"])

    @pl.loop(0, layer.groups)
    def _(g):
        layer.attention(s, w, g)

    og_move.wait()
    layer.regroup(og_here, s["og"])
    zero = jnp.zeros((1, layer.width), F32)
    gain2 = lax.fori_loop(0, layer.groups, lambda g, c: layer.feed_forward(s, w, g, c), zero)
    layer.wide_parts(s, wide_ref)
    wide.start()
    first = max(1, layer.groups // 4)
    back = functools.partial(layer.attention_back, s, w)
    gain1 = lax.fori_loop(0, first, back, zero)
    wide.to_chips()
    gain1 = lax.fori_loop(first, layer.groups, back, gain1)
    layer.square_parts(s, square_ref)
    square.start()
    gains.value[0] = jnp.zeros_like(gains.value[0])
    gains.value[0, 0:1, :] = gain1
    gains.value[0, 1:2, :] = gain2
    gains.start(0)
    layer.ungroup(s["gh"], x_here)
    wide.to_spaces()
    square.to_chips()
    y_move.start(x_here, y_ref, y_sems, local.at[2], False)
    gains.value[1] = gains.finish(0)
    gains.start(1)
    wide.gather_spaces()
    square.to_spaces()
    gains.value[2] = gains.finish(1)
    gains.start(2)
    wide.gather_chips()
    square.gather_spaces()
    wide.gather_cores()
    square.gather_chips()
    gains_out[...] = gains.finish(2) * scale
    square.gather_cores()
    y_move.wait()
    wide.wait()
    square.wait()


def padded(rows, devices):
    unit = 16 * devices
    return -(-rows // unit) * unit


def on_device(x, og, g1, wq, wk, wv, wo, g2, wu, wd):
    groups, spaces = lax.axis_size("member"), lax.axis_size("space")
    own_members, own_patches, width = x.shape
    spread = own_patches // groups
    everyone = own_members * groups
    hidden = wu.shape[1]
    layer = Layer(everyone, spread, width, hidden)
    vmem = pl.BlockSpec(memory_space=pltpu.VMEM)
    limit = 62 * 2**20
    wide_rows = padded(2 * hidden, groups * spaces)
    square_rows = padded(4 * width, groups * spaces)
    chips = groups // 2
    scale = 1.0 / math.sqrt(everyone * own_patches * spaces)
    scratch = layer.scratch()
    back, wide, square, gains = pl.pallas_call(
        functools.partial(kernel, layer, scale, tuple(scratch)),
        out_shape=(
            jax.ShapeDtypeStruct(x.shape, BF16),
            jax.ShapeDtypeStruct((wide_rows, width), BF16),
            jax.ShapeDtypeStruct((square_rows, width), BF16),
            jax.ShapeDtypeStruct((8, width), F32),
        ),
        in_specs=[vmem] * 10,
        out_specs=(vmem,) * 4,
        scratch_shapes=[
            *scratch.values(),
            *[pltpu.VMEM((everyone, spread, width), BF16)] * 2,
            *[pltpu.SemaphoreType.DMA((2, groups))] * 3,
            pltpu.SemaphoreType.DMA((3,)),
            pltpu.VMEM((wide_rows, width), F32),
            pltpu.VMEM((square_rows, width), F32),
            *Total.scratch(wide_rows, width, chips, spaces, BF16),
            *Total.scratch(square_rows, width, chips, spaces, F32),
            *Gains.scratch(width, chips, spaces),
        ],
        compiler_params=pltpu.CompilerParams(
            vmem_limit_bytes=limit, collective_id=0, has_side_effects=True
        ),
    )(x, og, g1.reshape(1, width), wq, wk, wv, wo, g2.reshape(1, width), wu, wd)
    return finish(og, back, wide, square, gains, width, hidden)


def finish(og, back, wide, square, gains, width, hidden):
    input_grad = og.astype(F32) + back.astype(F32)
    wide, square = wide.astype(F32), square.astype(F32)
    up = wide[hidden : 2 * hidden].reshape(hidden // width, width, width)
    up = up.transpose(1, 0, 2).reshape(width, hidden)
    squares = [square[width * i : width * (i + 1)] for i in range(4)]
    return (input_grad, *squares, up, wide[:hidden], gains[0], gains[1])


def solution(mesh):
    spread = P("member", "space", None)
    return jax.shard_map(
        on_device,
        mesh=mesh,
        in_specs=(spread, spread) + (P(),) * 8,
        out_specs=(spread,) + (P(),) * 8,
        check_vma=False,
    )
```

```python
import functools
import math

import jax
import jax.numpy as jnp
from jax import lax
from jax.experimental import pallas as pl
from jax.experimental.pallas import tpu as pltpu
from jax.sharding import PartitionSpec as P

HEAD_DIM = 32
EPS = 1e-06
GELU_C = 0.7978845608028654
GELU_A = 0.044715
F32 = jnp.float32
BF16 = jnp.bfloat16


def dot(left, right):
    return lax.dot_general(left, right, (((1,), (0,)), ((), ())), preferred_element_type=F32)


def dot_nt(left, right):
    return lax.dot_general(left, right, (((1,), (1,)), ((), ())), preferred_element_type=F32)


def dot_tn(left, right):
    return lax.dot_general(left, right, (((0,), (0,)), ((), ())), preferred_element_type=F32)


def norm_rows(values):
    inverse = lax.rsqrt(jnp.mean(values * values, axis=-1, keepdims=True) + EPS)
    return values * inverse, inverse


def norm_back(unit_rows, inverse, gains, upstream):
    scaled = upstream * gains
    return inverse * (scaled - unit_rows * jnp.mean(scaled * unit_rows, axis=-1, keepdims=True))


def gelu_pair(preact):
    square = preact * preact
    tangent = jnp.tanh(GELU_C * (preact + GELU_A * preact * square))
    half = 0.5 * (1.0 + tangent)
    slopes = half + 0.5 * preact * (1.0 - tangent * tangent) * (
        GELU_C + (3.0 * GELU_A * GELU_C) * square
    )
    return preact * half, slopes


class Layer:
    def __init__(self, members, patches, width, hidden):
        self.members, self.patches, self.width, self.hidden = members, patches, width, hidden
        self.heads = width // HEAD_DIM
        self.groups, self.rows = patches // 8, members * 8
        self.tokens = self.groups * self.rows
        self.scale = 1.0 / math.sqrt(HEAD_DIM)

    def scratch(self):
        groups, rows, width, hidden = self.groups, self.rows, self.width, self.hidden
        return dict(
            x=pltpu.VMEM((groups, rows, width), F32),
            og=pltpu.VMEM((groups, rows, width), BF16),
            n1=pltpu.VMEM((groups, rows, width), BF16),
            q=pltpu.VMEM((groups, rows, width), BF16),
            k=pltpu.VMEM((groups, rows, width), BF16),
            v=pltpu.VMEM((groups, rows, width), BF16),
            mix=pltpu.VMEM((groups, rows, width), BF16),
            n2=pltpu.VMEM((groups, rows, width), BF16),
            act=pltpu.VMEM((groups, rows, hidden), BF16),
            pre=pltpu.VMEM((groups, rows, hidden), BF16),
            ga=pltpu.VMEM((groups, rows, width), BF16),
            gm=pltpu.VMEM((groups, rows, width), BF16),
            gh=pltpu.VMEM((groups, rows, width), F32),
            p=pltpu.VMEM((groups, self.heads, rows, rows), F32),
        )

    def head_mask(self, head):
        lanes = lax.broadcasted_iota(jnp.int32, (1, self.width), 1)
        inside = (lanes >= head * HEAD_DIM) & (lanes < (head + 1) * HEAD_DIM)
        return jnp.where(inside, 1.0, 0.0).astype(BF16)

    def regroup(self, pair, source, target):
        block = source[:, 16 * pair : 16 * pair + 16, :].astype(F32)
        for half in range(2):
            piece = block[:, 8 * half : 8 * half + 8, :].reshape(self.rows, self.width)
            target[2 * pair + half] = piece.astype(target.dtype)

    def ungroup(self, pair, source, target):
        halves = [source[2 * pair + half].reshape(self.members, 8, self.width) for half in range(2)]
        target[:, 16 * pair : 16 * pair + 16, :] = jnp.concatenate(halves, axis=1).astype(
            target.dtype
        )

    def attention(self, s, w, g):
        unit, _ = norm_rows(s["x"][g])
        normed = (unit * w["g1"][...]).astype(BF16)
        s["n1"][g] = normed
        query = dot(normed, w["wq"][...]).astype(BF16)
        keys = dot(normed, w["wk"][...]).astype(BF16)
        values = dot(normed, w["wv"][...]).astype(BF16)
        s["q"][g], s["k"][g], s["v"][g] = query, keys, values
        rows = self.rows
        same = (
            lax.broadcasted_iota(jnp.int32, (rows, rows), 0) % 8
            == lax.broadcasted_iota(jnp.int32, (rows, rows), 1) % 8
        )
        mixed = jnp.zeros((rows, self.width), F32)
        for head in range(self.heads):
            mask = self.head_mask(head)
            scores = jnp.where(same, dot_nt(query * mask, keys) * self.scale, -1e30)
            weights = jnp.exp(scores - jnp.max(scores, axis=-1, keepdims=True))
            weights = weights * (1.0 / jnp.sum(weights, axis=-1, keepdims=True))
            s["p"][g, head] = weights
            mixed += dot(weights.astype(BF16), values * mask)
        s["mix"][g] = mixed.astype(BF16)

    def feed_forward(self, s, w, g, gain2):
        mixed, out_grad = s["mix"][g], s["og"][g]
        state = s["x"][g] + dot(mixed, w["wo"][...])
        unit, inverse = norm_rows(state)
        normed = (unit * w["g2"][...]).astype(BF16)
        s["n2"][g] = normed
        grad_normed = jnp.zeros((self.rows, self.width), F32)
        step = 256
        for at in range(0, self.hidden, step):
            some = slice(at, at + step)
            activated, slopes = gelu_pair(dot(normed, w["wu"][:, some]))
            s["act"][g, :, some] = activated.astype(BF16)
            grad_pre = (dot_nt(out_grad, w["wd"][some, :]) * slopes).astype(BF16)
            s["pre"][g, :, some] = grad_pre
            grad_normed += dot_nt(grad_pre, w["wu"][:, some])
        grad_hidden = out_grad.astype(F32) + norm_back(unit, inverse, w["g2"][...], grad_normed)
        s["gh"][g] = grad_hidden
        grad_attn = grad_hidden.astype(BF16)
        s["ga"][g] = grad_attn
        s["gm"][g] = dot_nt(grad_attn, w["wo"][...]).astype(BF16)
        return gain2 + jnp.sum(grad_normed * unit, axis=0, keepdims=True)

    def attention_back(self, s, w, g, gain1):
        query, keys, values, upstream = s["q"][g], s["k"][g], s["v"][g], s["gm"][g]
        grad_q = jnp.zeros((self.rows, self.width), F32)
        grad_k, grad_v = grad_q, grad_q
        for head in range(self.heads):
            mask = self.head_mask(head)
            weights = s["p"][g, head]
            up = upstream * mask
            dprob = dot_nt(up, values)
            both = weights * dprob
            dscore = both - weights * jnp.sum(both, axis=-1, keepdims=True)
            dscore = (dscore * self.scale).astype(BF16)
            grad_v += dot_tn(weights.astype(BF16), up)
            grad_q += dot(dscore, keys * mask)
            grad_k += dot_tn(dscore, query * mask)
        grad_q, grad_k, grad_v = (grad.astype(BF16) for grad in (grad_q, grad_k, grad_v))
        s["q"][g], s["k"][g], s["v"][g] = grad_q, grad_k, grad_v
        grad_normed = (
            dot_nt(grad_q, w["wq"][...])
            + dot_nt(grad_k, w["wk"][...])
            + dot_nt(grad_v, w["wv"][...])
        )
        unit, inverse = norm_rows(s["x"][g])
        back = norm_back(unit, inverse, w["g1"][...], grad_normed)
        s["gh"][g] = (s["gh"][g] - s["og"][g].astype(F32)) + back
        return gain1 + jnp.sum(grad_normed * unit, axis=0, keepdims=True)

    def flat(self, s, name):
        array = s[name][...]
        return array.reshape(self.tokens, array.shape[-1])

    def wide_parts(self, s, parts):
        out_grad, normed = self.flat(s, "og"), self.flat(s, "n2")
        for at in range(0, self.hidden, 256):
            some = slice(at, at + 256)
            act = s["act"][:, :, some].reshape(self.tokens, 256)
            parts[some, :] = dot_tn(act, out_grad)
            pre = s["pre"][:, :, some].reshape(self.tokens, 256)
            parts[self.hidden + at : self.hidden + at + 256, :] = dot_tn(normed, pre)
        self.clear_rest(parts, 2 * self.hidden)

    def square_parts(self, s, parts):
        normed = self.flat(s, "n1")
        at = 0
        for name in ("q", "k", "v"):
            parts[at : at + self.width, :] = dot_tn(normed, self.flat(s, name))
            at += self.width
        parts[at : at + self.width, :] = dot_tn(self.flat(s, "mix"), self.flat(s, "ga"))
        self.clear_rest(parts, at + self.width)

    def clear_rest(self, parts, used):
        rest = parts.shape[0] - used
        if rest:
            parts[used:, :] = jnp.zeros((rest, self.width), F32)


WEIGHTS = ("g1", "wq", "wk", "wv", "wo", "g2", "wu", "wd")


class Ring:
    def __init__(self):
        self.member, self.space = lax.axis_index("member"), lax.axis_index("space")
        self.members, self.spaces = lax.axis_size("member"), lax.axis_size("space")
        self.chips = self.members // 2
        self.core = lax.rem(self.member, 2)
        self.chip = self.member // 2

    def member_peer(self, off):
        return lax.rem(self.member + off, self.members)

    def sibling(self):
        return self.member + 1 - 2 * self.core

    def chip_peer(self, off):
        return lax.rem(self.chip + off, self.chips)

    def space_peer(self, off):
        return lax.rem(self.space + off, self.spaces)

    def barrier(self, along_space):
        barrier = pltpu.get_barrier_semaphore()
        targets = [(self.member_peer(off), self.space) for off in range(1, self.members)]
        if along_space:
            targets += [(self.member, self.space_peer(off)) for off in range(1, self.spaces)]
        for target in targets:
            pl.semaphore_signal(
                barrier, inc=1, device_id=target, device_id_type=pl.DeviceIdType.MESH
            )
        pl.semaphore_wait(barrier, len(targets))


def send(source, target, sems, slot, device):
    copy = pltpu.make_async_remote_copy(
        src_ref=source,
        dst_ref=target,
        send_sem=sems.at[0, slot],
        recv_sem=sems.at[1, slot],
        device_id=device,
        device_id_type=pl.DeviceIdType.MESH,
    )
    copy.start()
    return copy


def some_rows(start, size):
    return pl.ds(pl.multiple_of(start, 16), size)


class Exchange:
    def __init__(self, ring, own, spread, pair):
        self.ring, self.own, self.spread, self.pair = ring, own, spread, pair

    def mine(self, ref, index):
        return ref.at[:, some_rows(index * self.spread + 16 * self.pair, 16), :]

    def here(self, ref, index):
        return ref.at[pl.ds(index * self.own, self.own), pl.ds(16 * self.pair, 16), :]

    def start(self, source, target, sems, local, to_patch):
        ring = self.ring
        take, put = (self.mine, self.here) if to_patch else (self.here, self.mine)
        self.copies = []
        for off in range(1, ring.members):
            peer = ring.member_peer(off)
            self.copies.append(
                send(
                    take(source, peer),
                    put(target, ring.member),
                    sems.at[self.pair],
                    off,
                    (peer, ring.space),
                )
            )
        own = pltpu.make_async_copy(
            take(source, ring.member), put(target, ring.member), local.at[self.pair]
        )
        own.start()
        self.copies.append(own)
        return self

    def wait(self):
        for copy in self.copies:
            copy.wait()


class Total:
    def __init__(self, ring, scale, parts, full, recv_a, recv_b, recv_c, own, sems):
        self.ring, self.scale = ring, scale
        self.parts, self.full, self.sems, self.own = parts, full, sems, own
        self.recv_a, self.recv_b, self.recv_c = recv_a, recv_b, recv_c
        self.rows_a = parts.shape[0] // 2
        self.rows_b = self.rows_a // ring.chips
        self.rows_c = self.rows_b // ring.spaces
        self.at_a = ring.core * self.rows_a
        self.at_b = self.at_a + ring.chip * self.rows_b
        self.at_c = self.at_b + ring.space * self.rows_c

    @staticmethod
    def scratch(rows, width, chips, spaces):
        a = rows // 2
        b = a // chips
        c = b // spaces
        slots = 2 * (chips + spaces)
        return [
            pltpu.VMEM((a, width), F32),
            pltpu.VMEM((chips, b, width), F32),
            pltpu.VMEM((spaces, c, width), F32),
            pltpu.VMEM((b, width), F32),
            pltpu.SemaphoreType.DMA((2, slots)),
        ]

    def start(self):
        ring = self.ring
        other = some_rows((1 - ring.core) * self.rows_a, self.rows_a)
        self.copies = [
            send(self.parts.at[other], self.recv_a, self.sems, 0, (ring.sibling(), ring.space))
        ]

    def wait(self):
        for copy in self.copies:
            copy.wait()

    def to_chips(self):
        ring = self.ring
        self.wait()
        self.copies = []
        for off in range(1, ring.chips):
            peer = ring.chip_peer(off)
            at = peer * self.rows_b
            rows = some_rows(at, self.rows_b)
            place = some_rows(self.at_a + at, self.rows_b)
            self.parts[place, :] = self.parts[place, :] + self.recv_a[rows, :]
            device = (2 * peer + ring.core, ring.space)
            self.copies.append(
                send(self.parts.at[place], self.recv_b.at[off], self.sems, off, device)
            )
        mine = some_rows(ring.chip * self.rows_b, self.rows_b)
        self.own[...] = self.parts[some_rows(self.at_b, self.rows_b), :] + self.recv_a[mine, :]

    def to_spaces(self):
        ring = self.ring
        self.wait()
        self.copies = []
        total = self.own[...]
        for off in range(1, ring.chips):
            total += self.recv_b[off]
        self.own[...] = total
        for off in range(1, ring.spaces):
            peer = ring.space_peer(off)
            rows = some_rows(peer * self.rows_c, self.rows_c)
            slot = ring.chips + off
            self.copies.append(
                send(self.own.at[rows], self.recv_c.at[off], self.sems, slot, (ring.member, peer))
            )

    def gather_spaces(self):
        ring = self.ring
        self.wait()
        total = self.own[some_rows(ring.space * self.rows_c, self.rows_c), :]
        for off in range(1, ring.spaces):
            total += self.recv_c[off]
        rows = some_rows(self.at_c, self.rows_c)
        self.full[rows, :] = (total * self.scale).astype(BF16)
        place = self.full.at[rows]
        base = ring.chips + ring.spaces
        self.copies = [
            send(place, place, self.sems, base + off, (ring.member, ring.space_peer(off)))
            for off in range(1, ring.spaces)
        ]

    def gather_chips(self):
        ring = self.ring
        self.wait()
        place = self.full.at[some_rows(self.at_b, self.rows_b)]
        base = ring.chips + 2 * ring.spaces
        self.copies = [
            send(
                place, place, self.sems, base + off, (2 * ring.chip_peer(off) + ring.core, ring.space)
            )
            for off in range(1, ring.chips)
        ]

    def gather_cores(self):
        ring = self.ring
        self.wait()
        place = self.full.at[some_rows(self.at_a, self.rows_a)]
        slot = ring.chips + 2 * ring.spaces
        self.copies = [send(place, place, self.sems, slot, (ring.sibling(), ring.space))]


class Gains:
    def __init__(self, ring, value, recv, sems):
        self.ring, self.value, self.recv, self.sems = ring, value, recv, sems

    @staticmethod
    def scratch(width, chips, spaces):
        return [
            pltpu.VMEM((3, 8, width), F32),
            pltpu.VMEM((chips + spaces, 8, width), F32),
            pltpu.SemaphoreType.DMA((2, chips + spaces)),
        ]

    def peers(self, stage):
        ring = self.ring
        if stage == 0:
            return [(0, (ring.sibling(), ring.space))]
        if stage == 1:
            return [
                (off, (2 * ring.chip_peer(off) + ring.core, ring.space))
                for off in range(1, ring.chips)
            ]
        return [
            (ring.chips + off, (ring.member, ring.space_peer(off)))
            for off in range(1, ring.spaces)
        ]

    def start(self, stage):
        self.copies = [
            send(self.value.at[stage], self.recv.at[slot], self.sems, slot, device)
            for slot, device in self.peers(stage)
        ]

    def finish(self, stage):
        for copy in self.copies:
            copy.wait()
        total = self.value[stage]
        for slot, _ in self.peers(stage):
            total += self.recv[slot]
        return total


def kernel(layer, scale, names, *refs):
    x_ref, og_ref = refs[:2]
    w = dict(zip(WEIGHTS, refs[2:10]))
    y_ref, wide_out, square_out, gains_out = refs[10:14]
    s = dict(zip(names, refs[14:]))
    rest = refs[14 + len(names) :]
    x_here, og_here, x_sems, og_sems, y_sems, local, wide_ref, square_ref = rest[:8]
    ring = Ring()
    wide = Total(ring, scale, wide_ref, wide_out, *rest[8:13])
    square = Total(ring, scale, square_ref, square_out, *rest[13:18])
    gains = Gains(ring, *rest[18:21])
    own, spread = x_ref.shape[0], layer.patches
    pairs = layer.groups // 2
    x_moves, og_moves, y_moves = (
        [Exchange(ring, own, spread, pair) for pair in range(pairs)] for _ in range(3)
    )

    ring.barrier(True)
    for move in x_moves:
        move.start(x_ref, x_here, x_sems, local.at[0], True)
    for pair in range(pairs):
        x_moves[pair].wait()
        og_moves[pair].start(og_ref, og_here, og_sems, local.at[1], True)
        layer.regroup(pair, x_here, s["x"])

        @pl.loop(2 * pair, 2 * pair + 2)
        def _(g):
            layer.attention(s, w, g)

    zero = jnp.zeros((1, layer.width), F32)
    gain1 = gain2 = zero
    for pair in range(pairs):
        og_moves[pair].wait()
        layer.regroup(pair, og_here, s["og"])
        gain2 = lax.fori_loop(
            2 * pair, 2 * pair + 2, lambda g, c: layer.feed_forward(s, w, g, c), gain2
        )
    layer.wide_parts(s, wide_ref)
    wide.start()
    for g in range(layer.groups):
        gain1 = layer.attention_back(s, w, g, gain1)
        if g == 0:
            wide.to_chips()
        if g % 2 == 1:
            layer.ungroup(g // 2, s["gh"], x_here)
            y_moves[g // 2].start(x_here, y_ref, y_sems, local.at[2], False)
    layer.square_parts(s, square_ref)
    square.start()
    gains.value[0] = jnp.zeros_like(gains.value[0])
    gains.value[0, 0:1, :] = gain1
    gains.value[0, 1:2, :] = gain2
    gains.start(0)
    wide.to_spaces()
    square.to_chips()
    gains.value[1] = gains.finish(0)
    gains.start(1)
    wide.gather_spaces()
    wide.gather_chips()
    square.to_spaces()
    gains.value[2] = gains.finish(1)
    gains.start(2)
    square.gather_spaces()
    wide.gather_cores()
    square.gather_chips()
    gains_out[...] = gains.finish(2) * scale
    square.gather_cores()
    for move in y_moves:
        move.wait()
    wide.wait()
    square.wait()


def padded(rows, devices):
    unit = 16 * devices
    return -(-rows // unit) * unit


def on_device(x, og, g1, wq, wk, wv, wo, g2, wu, wd):
    groups, spaces = lax.axis_size("member"), lax.axis_size("space")
    own_members, own_patches, width = x.shape
    spread = own_patches // groups
    everyone = own_members * groups
    hidden = wu.shape[1]
    layer = Layer(everyone, spread, width, hidden)
    vmem = pl.BlockSpec(memory_space=pltpu.VMEM)
    limit = 62 * 2**20
    wide_rows = padded(2 * hidden, groups * spaces)
    square_rows = padded(4 * width, groups * spaces)
    chips = groups // 2
    scale = 1.0 / math.sqrt(everyone * own_patches * spaces)
    scratch = layer.scratch()
    back, wide, square, gains = pl.pallas_call(
        functools.partial(kernel, layer, scale, tuple(scratch)),
        out_shape=(
            jax.ShapeDtypeStruct(x.shape, BF16),
            jax.ShapeDtypeStruct((wide_rows, width), BF16),
            jax.ShapeDtypeStruct((square_rows, width), BF16),
            jax.ShapeDtypeStruct((8, width), F32),
        ),
        in_specs=[vmem] * 10,
        out_specs=(vmem,) * 4,
        scratch_shapes=[
            *scratch.values(),
            *[pltpu.VMEM((everyone, spread, width), BF16)] * 2,
            *[pltpu.SemaphoreType.DMA((spread // 16, 2, groups))] * 3,
            pltpu.SemaphoreType.DMA((3, spread // 16)),
            pltpu.VMEM((wide_rows, width), F32),
            pltpu.VMEM((square_rows, width), F32),
            *Total.scratch(wide_rows, width, chips, spaces),
            *Total.scratch(square_rows, width, chips, spaces),
            *Gains.scratch(width, chips, spaces),
        ],
        compiler_params=pltpu.CompilerParams(
            vmem_limit_bytes=limit, collective_id=0, has_side_effects=True
        ),
    )(x, og, g1.reshape(1, width), wq, wk, wv, wo, g2.reshape(1, width), wu, wd)
    return finish(og, back, wide, square, gains, width, hidden)


def finish(og, back, wide, square, gains, width, hidden):
    input_grad = og.astype(F32) + back.astype(F32)
    wide, square = wide.astype(F32), square.astype(F32)
    up = wide[hidden : 2 * hidden].reshape(hidden // width, width, width)
    up = up.transpose(1, 0, 2).reshape(width, hidden)
    squares = [square[width * i : width * (i + 1)] for i in range(4)]
    return (input_grad, *squares, up, wide[:hidden], gains[0], gains[1])


def solution(mesh):
    spread = P("member", "space", None)
    return jax.shard_map(
        on_device,
        mesh=mesh,
        in_specs=(spread, spread) + (P(),) * 8,
        out_specs=(spread,) + (P(),) * 8,
        check_vma=False,
    )
```
